32 devices in a mesh: groups: 2 (over y), vox: 4 (over z), sub: 2 (over x), map: 2 (over core).
Axes of the slice: x: 2, y: 2, z: 4, core: 2. Of those that a mesh axis runs over, the one named last changes fastest.
Arguments:
- data: bfloat16 [4, 256, 24576], P('groups', 'map', ('vox', 'sub')), parts along dimension 0, may hold values from -8 to 8
- maps: bfloat16 [400, 24576], P('groups', ('vox', 'sub')), parts along dimension 0, may hold values from -8 to 8
- neighbours: int32 [192, 4], P(('vox', 'sub')), may hold values from 0 to 191, as said below
- weights: float32 [4, 24576], P(None, ('vox', 'sub')), may hold values from 0.1 to 0.6
- noise_labels: int32 [128], P('groups'), parts along dimension 0, may hold values from 0 to 199, as said below
Outputs:
- clean: bfloat16 [4, 256, 24576], P('groups', 'map', ('vox', 'sub')), parts along dimension 0
The draws below stay inside these ranges and needn't reach their ends.
There are 2 independent parts, one for each index of `groups`. The reference program is written for one: setup_inputs(seed, part) draws one part's arguments, and reference() takes and returns one part's arrays. A program takes and returns all parts, laid end to end along the dimension named above; an argument that names none is the same for every part. Nothing has to cross between parts.
Inputs may be any that keep to these rules, and one draw needn't show every extreme that they name: `neighbours`: every entry is within 1 of its own block index; each block lists one neighbour 1 above and one 1 below, cut at the ends of the voxel range. `noise_labels`: distinct component indices.
All inputs are finite; a program needn't handle non-finite values.
Results may differ from the reference program's by a relative error of at most 0.0008.
The reference program's roundings to bfloat16 on the way (of `smoothed` and `noise_beta`) count: a program that leaves them out, or rounds other values in their place, can miss the bound.
Values may be sent and summed in bfloat16 or wider, within the bound.
A program may use at most 64 MiB of HBM per device.

```python
import math
import jax
import jax.numpy as jnp
from jax import lax

COMP = 200
NOISE = 64
SUBJ = 2
VOXBLK = 128
NEIGHBOUR_SLOTS = 4
NEIGHBOUR_REACH = 1
FRAMES = 256
VOXEL_BLOCKS = 192
VOXEL_COUNT = 24576


def joint_fields(key):
    key_base = jax.random.fold_in(key, 11)
    key_left = jax.random.fold_in(key, 13)
    key_right = jax.random.fold_in(key, 14)
    key_course = jax.random.fold_in(key, 15)
    key_noise = jax.random.fold_in(key, 16)
    base = jax.random.normal(key_base, (COMP, VOXEL_COUNT), jnp.float32)
    scale = jnp.ones((COMP, 1), jnp.float32)
    common = 0.5 * jax.random.normal(key_left, (1, VOXEL_COUNT), jnp.float32) * jax.random.normal(key_right, (COMP, 1), jnp.float32)
    maps = jnp.clip(base + common, -8.0, 8.0).astype(jnp.bfloat16)
    courses = jax.random.normal(key_course, (SUBJ, COMP, FRAMES), jnp.float32) / (math.sqrt(COMP) * scale[None])
    signal = jnp.einsum('cv,scf->sfv', maps.astype(jnp.float32), courses)
    noise = 0.5 * jax.random.normal(key_noise, (SUBJ, FRAMES, VOXEL_COUNT), jnp.float32)
    data = jnp.clip(signal + noise, -8.0, 8.0).astype(jnp.bfloat16)
    return (maps, data)


def draw_maps(key, part):
    return joint_fields(key)[0]


def draw_data(key, part):
    return joint_fields(key)[1]


def draw_neighbours(key, part):
    block_offsets = jax.random.randint(jax.random.fold_in(key, 21), (VOXEL_BLOCKS, NEIGHBOUR_SLOTS), -NEIGHBOUR_REACH, NEIGHBOUR_REACH + 1)
    block_offsets = block_offsets.at[:, 0].set(NEIGHBOUR_REACH).at[:, 1].set(-NEIGHBOUR_REACH)
    own = jnp.arange(VOXEL_BLOCKS, dtype=jnp.int32)[:, None]
    return jnp.clip(own + block_offsets, 0, VOXEL_BLOCKS - 1).astype(jnp.int32)


def draw_noise_labels(key, part):
    order = jax.random.permutation(jax.random.fold_in(key, 31), COMP)
    return order[:NOISE].astype(jnp.int32)


def level_of(rng, extent, cuts, smallest, high):
    def one(dim, parts):
        draws = jax.random.uniform(jax.random.fold_in(jax.random.fold_in(rng, 6), dim), (parts,), jnp.float32, smallest / len(cuts), high / len(cuts))
        return jnp.repeat(jnp.exp(draws), extent[dim] // parts).reshape((-1,) + (1,) * (len(extent) - dim - 1))

    loudness = one(*cuts[0])
    for cut in cuts[1:]:
        loudness = loudness * one(*cut)
    return loudness


def setup_inputs(seed: int = 0, part: int = 0) -> dict:
    seeds = jax.random.split(jax.random.key(seed), 6)
    part_splits = jax.random.split(jax.random.fold_in(seeds[5], part), 6)
    return {
        "data": draw_data(jax.random.fold_in(jax.random.fold_in(seeds[5], part), 71), part),
        "maps": draw_maps(jax.random.fold_in(jax.random.fold_in(seeds[5], part), 71), part),
        "neighbours": draw_neighbours(jax.random.fold_in(seeds[5], 71), part),
        "weights": jnp.clip(jnp.exp(math.log(0.6) - 1.7917595 * jax.random.uniform(seeds[3], (NEIGHBOUR_SLOTS, VOXEL_COUNT), jnp.float32) ** level_of(seeds[3], (NEIGHBOUR_SLOTS, VOXEL_COUNT), ((1, 8),), -0.2, 0.2)), 0.1, 0.6),
        "noise_labels": draw_noise_labels(jax.random.fold_in(jax.random.fold_in(seeds[5], part), 71), part),
    }


def solve_gram(gram, rhs):
    lower = jnp.linalg.cholesky(gram)
    half = lax.linalg.triangular_solve(lower, rhs, left_side=True, lower=True)
    return lax.linalg.triangular_solve(lower, half, left_side=True, lower=True, transpose_a=True)

def subject_smoothing(frames, neighbours, weights):
    blocks = frames.astype(jnp.float32).reshape(frames.shape[0], VOXEL_BLOCKS, VOXBLK)
    total = blocks
    for neighbour_slot in range(NEIGHBOUR_SLOTS):
        picked = jnp.take(blocks, neighbours[:, neighbour_slot], axis=1)
        total = total + weights[neighbour_slot].reshape(VOXEL_BLOCKS, VOXBLK) * picked
    return total.reshape(frames.shape[0], VOXEL_COUNT).astype(jnp.bfloat16)

def reference(data, maps, neighbours, weights, noise_labels):
    smoothed = lax.map(lambda frames: subject_smoothing(frames, neighbours, weights), data)
    gram = jnp.dot(maps.astype(jnp.float32), maps.T.astype(jnp.float32), preferred_element_type=jnp.float32)
    proj = lax.map(lambda frames: jnp.dot(maps.astype(jnp.float32), frames.T.astype(jnp.float32), preferred_element_type=jnp.float32), smoothed)
    rhs = jnp.transpose(proj, (1, 0, 2)).reshape(COMP, SUBJ * FRAMES)
    beta = solve_gram(gram, rhs)
    noise_beta = jnp.take(beta, noise_labels, axis=0).astype(jnp.bfloat16)
    noise_maps = jnp.take(maps, noise_labels, axis=0)
    courses = jnp.transpose(noise_beta.reshape(NOISE, SUBJ, FRAMES), (1, 0, 2))

    def clean_subject(pair):
        frames, course = pair
        fitted = jnp.dot(course.T.astype(jnp.float32), noise_maps.astype(jnp.float32), preferred_element_type=jnp.float32)
        return (frames.astype(jnp.float32) - fitted).astype(jnp.bfloat16)
    return lax.map(clean_subject, (smoothed, courses))
```

```python
import functools
import jax
import jax.numpy as jnp
from jax import lax
from jax.experimental import pallas as pl
from jax.experimental.pallas import tpu as pltpu
from jax.sharding import PartitionSpec as P

VOXBLK = 128
NEIGHBOUR_REACH = 1
MESH = pl.DeviceIdType.MESH
HIGHEST = lax.Precision.HIGHEST
NN = (((1,), (0,)), ((), ()))
NT = (((1,), (1,)), ((), ()))
TN = (((0,), (0,)), ((), ()))


def f32_dot(a, b, dims):
    return lax.dot_general(a, b, dims, precision=HIGHEST, preferred_element_type=jnp.float32)


def negative_inverse_small(block):
    size = block.shape[0]
    row_id = lax.broadcasted_iota(jnp.int32, (size, size), 0)
    col_id = lax.broadcasted_iota(jnp.int32, (size, size), 1)
    for k in range(size):
        pivot = block[k : k + 1, k : k + 1]
        row = jnp.where(col_id[:1] == k, -1.0, block[k : k + 1, :])
        col = jnp.where(row_id[:, :1] == k, -1.0, block[:, k : k + 1])
        rest = jnp.where((row_id == k) | (col_id == k), 0.0, block)
        block = rest - col * (row * (1.0 / pivot))
    return block


def negative_inverse(gram_ref, work_ref, size, step):
    row_id = lax.broadcasted_iota(jnp.int32, (size, size), 0)
    col_id = lax.broadcasted_iota(jnp.int32, (size, size), 1)
    own_row = lax.broadcasted_iota(jnp.int32, (step, size), 0)
    own_col = lax.broadcasted_iota(jnp.int32, (step, size), 1)
    work_ref[...] = gram_ref[pl.ds(0, size), :]
    for first in range(0, size, step):
        rows = work_ref[pl.ds(first, step), :]
        select = (own_col == own_row + first).astype(jnp.float32)
        small = negative_inverse_small(f32_dot(rows, select, NT))
        in_cols = (own_col >= first) & (own_col < first + step)
        turned = jnp.where(in_cols, -select, rows)
        update = f32_dot(turned, f32_dot(small, turned, NN), TN)
        inside = ((row_id >= first) & (row_id < first + step)) | (
            (col_id >= first) & (col_id < first + step)
        )
        work_ref[...] = jnp.where(inside, 0.0, work_ref[...]) + update


def kernel(
    count, sub_count, share, gram_share, step,
    data_ref, maps_ref, coef_ref, keep_ref,
    smooth_ref, beta_ref,
    low_ref, high_ref, gram_part, gram_in, gram_all, proj_part, proj_in, work_ref, beta_all,
    halo_send, halo_recv, gsend, grecv, asend, arecv, psend, precv, bsend, brecv,
):
    comps, width = maps_ref.shape
    blocks = width // VOXBLK
    me = lax.axis_index("vox") * sub_count + lax.axis_index("sub")

    def peer(k):
        return lax.rem(me + k, count)

    def device(index):
        return {"vox": lax.div(index, sub_count), "sub": lax.rem(index, sub_count)}

    def send(src, dst, send_sem, recv_sem, index):
        copy = pltpu.make_async_remote_copy(
            src_ref=src, dst_ref=dst, send_sem=send_sem, recv_sem=recv_sem,
            device_id=device(index), device_id_type=MESH,
        )
        copy.start()
        return copy

    def part(index, size, align):
        return pl.ds(pl.multiple_of(index * size, align), size)

    barrier = pltpu.get_barrier_semaphore()
    for k in range(1, count):
        pl.semaphore_signal(barrier, inc=1, device_id=device(peer(k)), device_id_type=MESH)
    pl.semaphore_wait(barrier, count - 1)

    halo = [
        send(data_ref.at[:, pl.ds(width - VOXBLK, VOXBLK)], low_ref,
             halo_send.at[0], halo_recv.at[0], peer(1)),
        send(data_ref.at[:, pl.ds(0, VOXBLK)], high_ref,
             halo_send.at[1], halo_recv.at[1], peer(count - 1)),
    ]

    maps = maps_ref[...]
    if gram_part.shape[0] > comps:
        gram_part[pl.ds(comps, gram_part.shape[0] - comps), :] = jnp.zeros(
            (gram_part.shape[0] - comps, comps), jnp.float32
        )
    gram_part[pl.ds(0, comps), :] = lax.dot_general(maps, maps, NT, preferred_element_type=jnp.float32)
    gram_copies = [
        send(gram_part.at[part(peer(k), gram_share, 8), :], gram_in.at[k], gsend.at[k], grecv.at[k], peer(k))
        for k in range(1, count)
    ]

    def columns(block):
        start = block * VOXBLK
        return pl.ds(start if isinstance(block, int) else pl.multiple_of(start, VOXBLK), VOXBLK)

    def smooth(block, low, high):
        here = columns(block)
        weight = coef_ref[:, here]
        total = data_ref[:, here].astype(jnp.float32) * weight[1:2]
        total = total + low.astype(jnp.float32) * weight[0:1] + high.astype(jnp.float32) * weight[2:3]
        smooth_ref[:, here] = total.astype(jnp.bfloat16)

    def inner(block, carry):
        smooth(block, data_ref[:, columns(block - 1)], data_ref[:, columns(block + 1)])
        return carry

    lax.fori_loop(1, blocks - 1, inner, 0)

    for copy in gram_copies:
        copy.wait()
    own = part(me, gram_share, 8)
    total = gram_part[own, :]
    for k in range(1, count):
        total = total + gram_in[k]
    gram_all[own, :] = total
    all_copies = [
        send(gram_all.at[own, :], gram_all.at[own, :], asend.at[k], arecv.at[k], peer(k))
        for k in range(1, count)
    ]

    for copy in halo:
        copy.wait()
    smooth(0, low_ref[...], data_ref[:, columns(1)])
    smooth(blocks - 1, data_ref[:, columns(blocks - 2)], high_ref[...])
    proj_part[...] = lax.dot_general(smooth_ref[...], maps, NT, preferred_element_type=jnp.float32)
    proj_copies = [
        send(proj_part.at[part(peer(k), share, 16), :], proj_in.at[k], psend.at[k], precv.at[k], peer(k))
        for k in range(1, count)
    ]

    for copy in all_copies:
        copy.wait()
    negative_inverse(gram_all, work_ref, comps, step)

    for copy in proj_copies:
        copy.wait()
    mine = part(me, share, 16)
    rhs = proj_part[mine, :]
    for k in range(1, count):
        rhs = rhs + proj_in[k]
    gram = gram_all[pl.ds(0, comps), :]
    beta = -f32_dot(rhs, work_ref[...], NN)
    left = rhs - f32_dot(beta, gram, NN)
    beta = beta - f32_dot(left, work_ref[...], NN)
    beta_all[mine, :] = jnp.where(keep_ref[...] > 0.0, beta, 0.0).astype(jnp.bfloat16)
    beta_copies = [
        send(beta_all.at[mine, :], beta_all.at[mine, :], bsend.at[k], brecv.at[k], peer(k))
        for k in range(1, count)
    ]
    for copy in beta_copies:
        copy.wait()
    beta_ref[...] = beta_all[...]


def fused(frames, maps, coef, keep, count, sub_count):
    rows, width = frames.shape
    comps = maps.shape[0]
    share = rows // count
    gram_share = 8 * (-(-comps // (8 * count)))
    step = next(size for size in (40, 32, 24, 16, 8) if comps % size == 0)
    f32, bf16 = jnp.float32, jnp.bfloat16
    vmem = pl.BlockSpec(memory_space=pltpu.VMEM)
    sems = pltpu.SemaphoreType.DMA((count,))
    return pl.pallas_call(
        functools.partial(kernel, count, sub_count, share, gram_share, step),
        out_shape=(
            jax.ShapeDtypeStruct((rows, width), bf16),
            jax.ShapeDtypeStruct((rows, comps), bf16),
        ),
        in_specs=[vmem] * 4,
        out_specs=(vmem, vmem),
        scratch_shapes=[
            pltpu.VMEM((rows, VOXBLK), bf16),
            pltpu.VMEM((rows, VOXBLK), bf16),
            pltpu.VMEM((count * gram_share, comps), f32),
            pltpu.VMEM((count, gram_share, comps), f32),
            pltpu.VMEM((count * gram_share, comps), f32),
            pltpu.VMEM((rows, comps), f32),
            pltpu.VMEM((count, share, comps), f32),
            pltpu.VMEM((comps, comps), f32),
            pltpu.VMEM((rows, comps), bf16),
            pltpu.SemaphoreType.DMA((2,)),
            pltpu.SemaphoreType.DMA((2,)),
            sems, sems, sems, sems, sems, sems, sems, sems,
        ],
        compiler_params=pltpu.CompilerParams(
            collective_id=0, has_side_effects=True, vmem_limit_bytes=48 * 1024 * 1024
        ),
    )(frames, maps, coef, keep)


def solve_gram(gram, rhs):
    lower = jnp.linalg.cholesky(gram)
    half = lax.linalg.triangular_solve(lower, rhs, left_side=True, lower=True)
    return lax.linalg.triangular_solve(lower, half, left_side=True, lower=True, transpose_a=True)


def by_collectives(frames, maps, coef, keep, count):
    forward = [(i, (i + 1) % count) for i in range(count)]
    backward = [(target, source) for source, target in forward]
    low = lax.ppermute(frames[:, -VOXBLK:], ("vox", "sub"), forward)
    high = lax.ppermute(frames[:, :VOXBLK], ("vox", "sub"), backward)
    below = jnp.concatenate([low, frames[:, :-VOXBLK]], axis=1).astype(jnp.float32)
    above = jnp.concatenate([frames[:, VOXBLK:], high], axis=1).astype(jnp.float32)
    smoothed = frames.astype(jnp.float32) * coef[1:2] + below * coef[0:1] + above * coef[2:3]
    smoothed = smoothed.astype(jnp.bfloat16)
    gram = lax.dot_general(maps, maps, NT, preferred_element_type=jnp.float32)
    proj = lax.dot_general(maps, smoothed, NT, preferred_element_type=jnp.float32)
    gram, proj = lax.psum((gram, proj), ("vox", "sub"))
    beta = solve_gram(gram, proj).T
    return smoothed, jnp.where(keep > 0.0, beta, 0.0).astype(jnp.bfloat16)


def local(data, maps, neighbours, weights, noise_labels):
    subjects, frames, width = data.shape
    comps = maps.shape[0]
    blocks = width // VOXBLK
    rows = subjects * frames
    sub_count = lax.axis_size("sub")
    count = lax.axis_size("vox") * sub_count
    own = lax.axis_index(("vox", "sub")) * blocks + jnp.arange(blocks, dtype=jnp.int32)
    offset = (neighbours - own[:, None]).T[:, :, None]
    slots = weights.reshape(weights.shape[0], blocks, VOXBLK)
    coef = jnp.stack(
        [
            jnp.sum(jnp.where(offset == reach, slots, 0.0), axis=0) + (1.0 if reach == 0 else 0.0)
            for reach in range(-NEIGHBOUR_REACH, NEIGHBOUR_REACH + 1)
        ]
    ).reshape(2 * NEIGHBOUR_REACH + 1, width)
    labels = lax.broadcasted_iota(jnp.int32, (noise_labels.shape[0], comps), 1)
    keep = jnp.max((labels == noise_labels[:, None]).astype(jnp.float32), axis=0, keepdims=True)
    stacked = data.reshape(rows, width)
    if rows % (16 * count) == 0 and count <= 16 and blocks > 2:
        smoothed, beta = fused(stacked, maps, coef, keep, count, sub_count)
    else:
        smoothed, beta = by_collectives(stacked, maps, coef, keep, count)
    fitted = jnp.einsum("rc,cv->rv", beta, maps, preferred_element_type=jnp.float32)
    clean = (smoothed.astype(jnp.float32) - fitted).astype(jnp.bfloat16)
    return clean.reshape(subjects, frames, width)


def solution(mesh):
    return jax.shard_map(
        local,
        mesh=mesh,
        in_specs=(
            P("groups", "map", ("vox", "sub")),
            P("groups", ("vox", "sub")),
            P(("vox", "sub"), None),
            P(None, ("vox", "sub")),
            P("groups"),
        ),
        out_specs=P("groups", "map", ("vox", "sub")),
        check_vma=False,
    )
```

```python
import functools
import jax
import jax.numpy as jnp
from jax import lax
from jax.experimental import pallas as pl
from jax.experimental.pallas import tpu as pltpu
from jax.sharding import PartitionSpec as P

VOXBLK = 128
NEIGHBOUR_REACH = 1
PIVOTS = 8
MESH = pl.DeviceIdType.MESH
HIGHEST = lax.Precision.HIGHEST
NN = (((1,), (0,)), ((), ()))
NT = (((1,), (1,)), ((), ()))
TN = (((0,), (0,)), ((), ()))


def f32_dot(a, b, dims):
    return lax.dot_general(a, b, dims, precision=HIGHEST, preferred_element_type=jnp.float32)


def swept(entries, size):
    def at(i, j):
        return entries[(min(i, j), max(i, j))]

    for p in range(size):
        inverse = 1.0 / at(p, p)
        scaled = {i: at(i, p) * inverse for i in range(size) if i != p}
        later = {}
        for i in range(size):
            for j in range(i, size):
                if i == p and j == p:
                    later[(i, j)] = -inverse
                elif i == p:
                    later[(i, j)] = scaled[j]
                elif j == p:
                    later[(i, j)] = scaled[i]
                else:
                    later[(i, j)] = at(i, j) - at(i, p) * scaled[j]
        entries = later
    return entries


def negative_inverse_small(block):
    size = block.shape[0]
    row_id = lax.broadcasted_iota(jnp.int32, (size, size), 0)
    col_id = lax.broadcasted_iota(jnp.int32, (size, size), 1)
    for first in range(0, size, PIVOTS):
        group = range(PIVOTS)
        cols = [jnp.broadcast_to(block[:, first + j : first + j + 1], (size, size)) for j in group]
        rows = [block[first + i : first + i + 1, :] for i in group]
        upper = {(i, j): cols[j][first + i : first + i + 1, :] for i in group for j in group if i <= j}
        pivots = swept(upper, PIVOTS)
        in_rows = (row_id >= first) & (row_id < first + PIVOTS)
        in_cols = (col_id >= first) & (col_id < first + PIVOTS)
        rows = [
            jnp.where(col_id[:1] == first + i, -1.0, jnp.where(in_cols[:1], 0.0, rows[i])) for i in group
        ]
        cols = [jnp.where(row_id == first + i, -1.0, jnp.where(in_rows, 0.0, cols[i])) for i in group]
        block = jnp.where(in_rows | in_cols, 0.0, block)
        for i in group:
            mixed = pivots[(0, i)] * rows[0]
            for j in group[1:]:
                mixed = mixed + pivots[(min(i, j), max(i, j))] * rows[j]
            block = block + cols[i] * mixed
    return block


def negative_inverse(gram_ref, work_ref, size, step):
    row_id = lax.broadcasted_iota(jnp.int32, (size, size), 0)
    col_id = lax.broadcasted_iota(jnp.int32, (size, size), 1)
    own_row = lax.broadcasted_iota(jnp.int32, (step, size), 0)
    own_col = lax.broadcasted_iota(jnp.int32, (step, size), 1)
    work_ref[...] = gram_ref[pl.ds(0, size), :]
    for first in range(0, size, step):
        rows = work_ref[pl.ds(first, step), :]
        select = (own_col == own_row + first).astype(jnp.float32)
        small = negative_inverse_small(rows[:, first : first + step])
        in_cols = (own_col >= first) & (own_col < first + step)
        turned = jnp.where(in_cols, -select, rows)
        update = f32_dot(turned, f32_dot(small, turned, NN), TN)
        inside = ((row_id >= first) & (row_id < first + step)) | (
            (col_id >= first) & (col_id < first + step)
        )
        work_ref[...] = jnp.where(inside, 0.0, work_ref[...]) + update


def kernel(
    count, sub_count, share, gram_share, step,
    data_ref, maps_ref, coef_ref, keep_ref,
    smooth_ref, beta_ref,
    low_ref, high_ref, gram_part, gram_in, gram_all, proj_part, proj_in, work_ref, beta_all,
    halo_send, halo_recv, gsend, grecv, asend, arecv, psend, precv, bsend, brecv,
):
    comps, width = maps_ref.shape
    blocks = width // VOXBLK
    me = lax.axis_index("vox") * sub_count + lax.axis_index("sub")

    def peer(k):
        return lax.rem(me + k, count)

    def device(index):
        return {"vox": lax.div(index, sub_count), "sub": lax.rem(index, sub_count)}

    def send(src, dst, send_sem, recv_sem, index):
        copy = pltpu.make_async_remote_copy(
            src_ref=src, dst_ref=dst, send_sem=send_sem, recv_sem=recv_sem,
            device_id=device(index), device_id_type=MESH,
        )
        copy.start()
        return copy

    def part(index, size, align):
        return pl.ds(pl.multiple_of(index * size, align), size)

    barrier = pltpu.get_barrier_semaphore()
    for k in range(1, count):
        pl.semaphore_signal(barrier, inc=1, device_id=device(peer(k)), device_id_type=MESH)
    pl.semaphore_wait(barrier, count - 1)

    halo = [
        send(data_ref.at[:, pl.ds(width - VOXBLK, VOXBLK)], low_ref,
             halo_send.at[0], halo_recv.at[0], peer(1)),
        send(data_ref.at[:, pl.ds(0, VOXBLK)], high_ref,
             halo_send.at[1], halo_recv.at[1], peer(count - 1)),
    ]

    maps = maps_ref[...]
    if gram_part.shape[0] > comps:
        gram_part[pl.ds(comps, gram_part.shape[0] - comps), :] = jnp.zeros(
            (gram_part.shape[0] - comps, comps), jnp.float32
        )
    gram_part[pl.ds(0, comps), :] = lax.dot_general(maps, maps, NT, preferred_element_type=jnp.float32)
    gram_copies = [
        send(gram_part.at[part(peer(k), gram_share, 8), :], gram_in.at[k], gsend.at[k], grecv.at[k], peer(k))
        for k in range(1, count)
    ]

    def columns(block):
        start = block * VOXBLK
        return pl.ds(start if isinstance(block, int) else pl.multiple_of(start, VOXBLK), VOXBLK)

    def smooth(block, low, high):
        here = columns(block)
        weight = coef_ref[:, here]
        total = data_ref[:, here].astype(jnp.float32) * weight[1:2]
        total = total + low.astype(jnp.float32) * weight[0:1] + high.astype(jnp.float32) * weight[2:3]
        smooth_ref[:, here] = total.astype(jnp.bfloat16)

    def inner(block, carry):
        smooth(block, data_ref[:, columns(block - 1)], data_ref[:, columns(block + 1)])
        return carry

    lax.fori_loop(1, blocks - 1, inner, 0)

    for copy in gram_copies:
        copy.wait()
    own = part(me, gram_share, 8)
    total = gram_part[own, :]
    for k in range(1, count):
        total = total + gram_in[k]
    gram_all[own, :] = total
    all_copies = [
        send(gram_all.at[own, :], gram_all.at[own, :], asend.at[k], arecv.at[k], peer(k))
        for k in range(1, count)
    ]

    for copy in halo:
        copy.wait()
    smooth(0, low_ref[...], data_ref[:, columns(1)])
    smooth(blocks - 1, data_ref[:, columns(blocks - 2)], high_ref[...])
    proj_part[...] = lax.dot_general(smooth_ref[...], maps, NT, preferred_element_type=jnp.float32)
    proj_copies = [
        send(proj_part.at[part(peer(k), share, 16), :], proj_in.at[k], psend.at[k], precv.at[k], peer(k))
        for k in range(1, count)
    ]

    for copy in all_copies:
        copy.wait()
    negative_inverse(gram_all, work_ref, comps, step)

    for copy in proj_copies:
        copy.wait()
    mine = part(me, share, 16)
    rhs = proj_part[mine, :]
    for k in range(1, count):
        rhs = rhs + proj_in[k]
    gram = gram_all[pl.ds(0, comps), :]
    beta = -f32_dot(rhs, work_ref[...], NN)
    left = rhs - f32_dot(beta, gram, NN)
    beta = beta - f32_dot(left, work_ref[...], NN)
    beta_all[mine, :] = jnp.where(keep_ref[...] > 0.0, beta, 0.0).astype(jnp.bfloat16)
    beta_copies = [
        send(beta_all.at[mine, :], beta_all.at[mine, :], bsend.at[k], brecv.at[k], peer(k))
        for k in range(1, count)
    ]
    for copy in beta_copies:
        copy.wait()
    beta_ref[...] = beta_all[...]


def fused(frames, maps, coef, keep, count, sub_count):
    rows, width = frames.shape
    comps = maps.shape[0]
    share = rows // count
    gram_share = 8 * (-(-comps // (8 * count)))
    step = next(size for size in (40, 32, 24, 16, 8) if comps % size == 0)
    f32, bf16 = jnp.float32, jnp.bfloat16
    vmem = pl.BlockSpec(memory_space=pltpu.VMEM)
    sems = pltpu.SemaphoreType.DMA((count,))
    return pl.pallas_call(
        functools.partial(kernel, count, sub_count, share, gram_share, step),
        out_shape=(
            jax.ShapeDtypeStruct((rows, width), bf16),
            jax.ShapeDtypeStruct((rows, comps), bf16),
        ),
        in_specs=[vmem] * 4,
        out_specs=(vmem, vmem),
        scratch_shapes=[
            pltpu.VMEM((rows, VOXBLK), bf16),
            pltpu.VMEM((rows, VOXBLK), bf16),
            pltpu.VMEM((count * gram_share, comps), f32),
            pltpu.VMEM((count, gram_share, comps), f32),
            pltpu.VMEM((count * gram_share, comps), f32),
            pltpu.VMEM((rows, comps), f32),
            pltpu.VMEM((count, share, comps), f32),
            pltpu.VMEM((comps, comps), f32),
            pltpu.VMEM((rows, comps), bf16),
            pltpu.SemaphoreType.DMA((2,)),
            pltpu.SemaphoreType.DMA((2,)),
            sems, sems, sems, sems, sems, sems, sems, sems,
        ],
        compiler_params=pltpu.CompilerParams(
            collective_id=0, has_side_effects=True, vmem_limit_bytes=48 * 1024 * 1024
        ),
    )(frames, maps, coef, keep)


def solve_gram(gram, rhs):
    lower = jnp.linalg.cholesky(gram)
    half = lax.linalg.triangular_solve(lower, rhs, left_side=True, lower=True)
    return lax.linalg.triangular_solve(lower, half, left_side=True, lower=True, transpose_a=True)


def by_collectives(frames, maps, coef, keep, count):
    forward = [(i, (i + 1) % count) for i in range(count)]
    backward = [(target, source) for source, target in forward]
    low = lax.ppermute(frames[:, -VOXBLK:], ("vox", "sub"), forward)
    high = lax.ppermute(frames[:, :VOXBLK], ("vox", "sub"), backward)
    below = jnp.concatenate([low, frames[:, :-VOXBLK]], axis=1).astype(jnp.float32)
    above = jnp.concatenate([frames[:, VOXBLK:], high], axis=1).astype(jnp.float32)
    smoothed = frames.astype(jnp.float32) * coef[1:2] + below * coef[0:1] + above * coef[2:3]
    smoothed = smoothed.astype(jnp.bfloat16)
    gram = lax.dot_general(maps, maps, NT, preferred_element_type=jnp.float32)
    proj = lax.dot_general(maps, smoothed, NT, preferred_element_type=jnp.float32)
    gram, proj = lax.psum((gram, proj), ("vox", "sub"))
    beta = solve_gram(gram, proj).T
    return smoothed, jnp.where(keep > 0.0, beta, 0.0).astype(jnp.bfloat16)


def local(data, maps, neighbours, weights, noise_labels):
    subjects, frames, width = data.shape
    comps = maps.shape[0]
    blocks = width // VOXBLK
    rows = subjects * frames
    sub_count = lax.axis_size("sub")
    count = lax.axis_size("vox") * sub_count
    own = lax.axis_index(("vox", "sub")) * blocks + jnp.arange(blocks, dtype=jnp.int32)
    offset = (neighbours - own[:, None]).T[:, :, None]
    slots = weights.reshape(weights.shape[0], blocks, VOXBLK)
    coef = jnp.stack(
        [
            jnp.sum(jnp.where(offset == reach, slots, 0.0), axis=0) + (1.0 if reach == 0 else 0.0)
            for reach in range(-NEIGHBOUR_REACH, NEIGHBOUR_REACH + 1)
        ]
    ).reshape(2 * NEIGHBOUR_REACH + 1, width)
    labels = lax.broadcasted_iota(jnp.int32, (noise_labels.shape[0], comps), 1)
    keep = jnp.max((labels == noise_labels[:, None]).astype(jnp.float32), axis=0, keepdims=True)
    stacked = data.reshape(rows, width)
    if rows % (16 * count) == 0 and count <= 16 and blocks > 2:
        smoothed, beta = fused(stacked, maps, coef, keep, count, sub_count)
    else:
        smoothed, beta = by_collectives(stacked, maps, coef, keep, count)
    fitted = jnp.einsum("rc,cv->rv", beta, maps, preferred_element_type=jnp.float32)
    clean = (smoothed.astype(jnp.float32) - fitted).astype(jnp.bfloat16)
    return clean.reshape(subjects, frames, width)


def solution(mesh):
    return jax.shard_map(
        local,
        mesh=mesh,
        in_specs=(
            P("groups", "map", ("vox", "sub")),
            P("groups", ("vox", "sub")),
            P(("vox", "sub"), None),
            P(None, ("vox", "sub")),
            P("groups"),
        ),
        out_specs=P("groups", "map", ("vox", "sub")),
        check_vma=False,
    )
```

```python
import functools
import jax
import jax.numpy as jnp
from jax import lax
from jax.experimental import pallas as pl
from jax.experimental.pallas import tpu as pltpu
from jax.sharding import PartitionSpec as P

VOXBLK = 128
NEIGHBOUR_REACH = 1
PIVOTS = 8
MESH = pl.DeviceIdType.MESH
HIGHEST = lax.Precision.HIGHEST
NN = (((1,), (0,)), ((), ()))
NT = (((1,), (1,)), ((), ()))
TN = (((0,), (0,)), ((), ()))


def f32_dot(a, b, dims):
    return lax.dot_general(a, b, dims, precision=HIGHEST, preferred_element_type=jnp.float32)


def swept(entries, size):
    def at(i, j):
        return entries[(min(i, j), max(i, j))]

    for p in range(size):
        inverse = 1.0 / at(p, p)
        scaled = {i: at(i, p) * inverse for i in range(size) if i != p}
        later = {}
        for i in range(size):
            for j in range(i, size):
                if i == p and j == p:
                    later[(i, j)] = -inverse
                elif i == p:
                    later[(i, j)] = scaled[j]
                elif j == p:
                    later[(i, j)] = scaled[i]
                else:
                    later[(i, j)] = at(i, j) - at(i, p) * scaled[j]
        entries = later
    return entries


def negative_inverse_small(block):
    size = block.shape[0]
    row_id = lax.broadcasted_iota(jnp.int32, (size, size), 0)
    col_id = lax.broadcasted_iota(jnp.int32, (size, size), 1)
    for first in range(0, size, PIVOTS):
        group = range(PIVOTS)
        cols = [jnp.broadcast_to(block[:, first + j : first + j + 1], (size, size)) for j in group]
        rows = [block[first + i : first + i + 1, :] for i in group]
        upper = {(i, j): cols[j][first + i : first + i + 1, :] for i in group for j in group if i <= j}
        pivots = swept(upper, PIVOTS)
        in_rows = (row_id >= first) & (row_id < first + PIVOTS)
        in_cols = (col_id >= first) & (col_id < first + PIVOTS)
        rows = [
            jnp.where(col_id[:1] == first + i, -1.0, jnp.where(in_cols[:1], 0.0, rows[i])) for i in group
        ]
        cols = [jnp.where(row_id == first + i, -1.0, jnp.where(in_rows, 0.0, cols[i])) for i in group]
        block = jnp.where(in_rows | in_cols, 0.0, block)
        for i in group:
            mixed = pivots[(0, i)] * rows[0]
            for j in group[1:]:
                mixed = mixed + pivots[(min(i, j), max(i, j))] * rows[j]
            block = block + cols[i] * mixed
    return block


def negative_inverse(gram_ref, work_ref, size, step):
    row_id = lax.broadcasted_iota(jnp.int32, (size, size), 0)
    col_id = lax.broadcasted_iota(jnp.int32, (size, size), 1)
    own_row = lax.broadcasted_iota(jnp.int32, (step, size), 0)
    own_col = lax.broadcasted_iota(jnp.int32, (step, size), 1)
    work_ref[...] = gram_ref[pl.ds(0, size), :]
    for first in range(0, size, step):
        rows = work_ref[pl.ds(first, step), :]
        select = (own_col == own_row + first).astype(jnp.float32)
        small = negative_inverse_small(rows[:, first : first + step])
        in_cols = (own_col >= first) & (own_col < first + step)
        turned = jnp.where(in_cols, -select, rows)
        update = f32_dot(turned, f32_dot(small, turned, NN), TN)
        inside = ((row_id >= first) & (row_id < first + step)) | (
            (col_id >= first) & (col_id < first + step)
        )
        work_ref[...] = jnp.where(inside, 0.0, work_ref[...]) + update


def kernel(
    count, sub_count, share, gram_share, step,
    data_hbm, maps_hbm, coef_ref, keep_ref,
    smooth_ref, beta_ref,
    data_ref, maps_ref, load_sems,
    low_ref, high_ref, gram_part, gram_in, gram_all, proj_part, proj_in, work_ref, beta_all,
    halo_send, halo_recv, gsend, grecv, asend, arecv, psend, precv, bsend, brecv,
):
    comps, width = maps_ref.shape
    blocks = width // VOXBLK
    me = lax.axis_index("vox") * sub_count + lax.axis_index("sub")

    def peer(k):
        return lax.rem(me + k, count)

    def device(index):
        return {"vox": lax.div(index, sub_count), "sub": lax.rem(index, sub_count)}

    def send(src, dst, send_sem, recv_sem, index):
        copy = pltpu.make_async_remote_copy(
            src_ref=src, dst_ref=dst, send_sem=send_sem, recv_sem=recv_sem,
            device_id=device(index), device_id_type=MESH,
        )
        copy.start()
        return copy

    def part(index, size, align):
        return pl.ds(pl.multiple_of(index * size, align), size)

    load_maps = pltpu.make_async_copy(maps_hbm, maps_ref, load_sems.at[0])
    load_data = pltpu.make_async_copy(data_hbm, data_ref, load_sems.at[1])
    load_maps.start()
    load_data.start()

    barrier = pltpu.get_barrier_semaphore()
    for k in range(1, count):
        pl.semaphore_signal(barrier, inc=1, device_id=device(peer(k)), device_id_type=MESH)
    pl.semaphore_wait(barrier, count - 1)

    load_maps.wait()
    maps = maps_ref[...]
    if gram_part.shape[0] > comps:
        gram_part[pl.ds(comps, gram_part.shape[0] - comps), :] = jnp.zeros(
            (gram_part.shape[0] - comps, comps), jnp.float32
        )
    gram_part[pl.ds(0, comps), :] = lax.dot_general(maps, maps, NT, preferred_element_type=jnp.float32)
    gram_copies = [
        send(gram_part.at[part(peer(k), gram_share, 8), :], gram_in.at[k], gsend.at[k], grecv.at[k], peer(k))
        for k in range(1, count)
    ]

    load_data.wait()
    halo = [
        send(data_ref.at[:, pl.ds(width - VOXBLK, VOXBLK)], low_ref,
             halo_send.at[0], halo_recv.at[0], peer(1)),
        send(data_ref.at[:, pl.ds(0, VOXBLK)], high_ref,
             halo_send.at[1], halo_recv.at[1], peer(count - 1)),
    ]

    def columns(block):
        start = block * VOXBLK
        return pl.ds(start if isinstance(block, int) else pl.multiple_of(start, VOXBLK), VOXBLK)

    def smooth(block, low, high):
        here = columns(block)
        weight = coef_ref[:, here]
        total = data_ref[:, here].astype(jnp.float32) * weight[1:2]
        total = total + low.astype(jnp.float32) * weight[0:1] + high.astype(jnp.float32) * weight[2:3]
        smooth_ref[:, here] = total.astype(jnp.bfloat16)

    def inner(block, carry):
        smooth(block, data_ref[:, columns(block - 1)], data_ref[:, columns(block + 1)])
        return carry

    lax.fori_loop(1, blocks - 1, inner, 0)

    for copy in gram_copies:
        copy.wait()
    own = part(me, gram_share, 8)
    total = gram_part[own, :]
    for k in range(1, count):
        total = total + gram_in[k]
    gram_all[own, :] = total
    all_copies = [
        send(gram_all.at[own, :], gram_all.at[own, :], asend.at[k], arecv.at[k], peer(k))
        for k in range(1, count)
    ]

    for copy in halo:
        copy.wait()
    smooth(0, low_ref[...], data_ref[:, columns(1)])
    smooth(blocks - 1, data_ref[:, columns(blocks - 2)], high_ref[...])
    proj_part[...] = lax.dot_general(smooth_ref[...], maps, NT, preferred_element_type=jnp.float32)
    proj_copies = [
        send(proj_part.at[part(peer(k), share, 16), :], proj_in.at[k], psend.at[k], precv.at[k], peer(k))
        for k in range(1, count)
    ]

    for copy in all_copies:
        copy.wait()
    negative_inverse(gram_all, work_ref, comps, step)

    for copy in proj_copies:
        copy.wait()
    mine = part(me, share, 16)
    rhs = proj_part[mine, :]
    for k in range(1, count):
        rhs = rhs + proj_in[k]
    gram = gram_all[pl.ds(0, comps), :]
    beta = -f32_dot(rhs, work_ref[...], NN)
    left = rhs - f32_dot(beta, gram, NN)
    beta = beta - f32_dot(left, work_ref[...], NN)
    beta_all[mine, :] = jnp.where(keep_ref[...] > 0.0, beta, 0.0).astype(jnp.bfloat16)
    beta_copies = [
        send(beta_all.at[mine, :], beta_all.at[mine, :], bsend.at[k], brecv.at[k], peer(k))
        for k in range(1, count)
    ]
    for copy in beta_copies:
        copy.wait()
    beta_ref[...] = beta_all[...]


def fused(frames, maps, coef, keep, count, sub_count):
    rows, width = frames.shape
    comps = maps.shape[0]
    share = rows // count
    gram_share = 8 * (-(-comps // (8 * count)))
    step = next(size for size in (40, 32, 24, 16, 8) if comps % size == 0)
    f32, bf16 = jnp.float32, jnp.bfloat16
    vmem = pl.BlockSpec(memory_space=pltpu.VMEM)
    hbm = pl.BlockSpec(memory_space=pltpu.HBM)
    sems = pltpu.SemaphoreType.DMA((count,))
    return pl.pallas_call(
        functools.partial(kernel, count, sub_count, share, gram_share, step),
        out_shape=(
            jax.ShapeDtypeStruct((rows, width), bf16),
            jax.ShapeDtypeStruct((rows, comps), bf16),
        ),
        in_specs=[hbm, hbm, vmem, vmem],
        out_specs=(vmem, vmem),
        scratch_shapes=[
            pltpu.VMEM((rows, width), bf16),
            pltpu.VMEM((comps, width), bf16),
            pltpu.SemaphoreType.DMA((2,)),
            pltpu.VMEM((rows, VOXBLK), bf16),
            pltpu.VMEM((rows, VOXBLK), bf16),
            pltpu.VMEM((count * gram_share, comps), f32),
            pltpu.VMEM((count, gram_share, comps), f32),
            pltpu.VMEM((count * gram_share, comps), f32),
            pltpu.VMEM((rows, comps), f32),
            pltpu.VMEM((count, share, comps), f32),
            pltpu.VMEM((comps, comps), f32),
            pltpu.VMEM((rows, comps), bf16),
            pltpu.SemaphoreType.DMA((2,)),
            pltpu.SemaphoreType.DMA((2,)),
            sems, sems, sems, sems, sems, sems, sems, sems,
        ],
        compiler_params=pltpu.CompilerParams(
            collective_id=0, has_side_effects=True, vmem_limit_bytes=60 * 1024 * 1024
        ),
    )(frames, maps, coef, keep)


def solve_gram(gram, rhs):
    lower = jnp.linalg.cholesky(gram)
    half = lax.linalg.triangular_solve(lower, rhs, left_side=True, lower=True)
    return lax.linalg.triangular_solve(lower, half, left_side=True, lower=True, transpose_a=True)


def by_collectives(frames, maps, coef, keep, count):
    forward = [(i, (i + 1) % count) for i in range(count)]
    backward = [(target, source) for source, target in forward]
    low = lax.ppermute(frames[:, -VOXBLK:], ("vox", "sub"), forward)
    high = lax.ppermute(frames[:, :VOXBLK], ("vox", "sub"), backward)
    below = jnp.concatenate([low, frames[:, :-VOXBLK]], axis=1).astype(jnp.float32)
    above = jnp.concatenate([frames[:, VOXBLK:], high], axis=1).astype(jnp.float32)
    smoothed = frames.astype(jnp.float32) * coef[1:2] + below * coef[0:1] + above * coef[2:3]
    smoothed = smoothed.astype(jnp.bfloat16)
    gram = lax.dot_general(maps, maps, NT, preferred_element_type=jnp.float32)
    proj = lax.dot_general(maps, smoothed, NT, preferred_element_type=jnp.float32)
    gram, proj = lax.psum((gram, proj), ("vox", "sub"))
    beta = solve_gram(gram, proj).T
    return smoothed, jnp.where(keep > 0.0, beta, 0.0).astype(jnp.bfloat16)


def local(data, maps, neighbours, weights, noise_labels):
    subjects, frames, width = data.shape
    comps = maps.shape[0]
    blocks = width // VOXBLK
    rows = subjects * frames
    sub_count = lax.axis_size("sub")
    count = lax.axis_size("vox") * sub_count
    own = lax.axis_index(("vox", "sub")) * blocks + jnp.arange(blocks, dtype=jnp.int32)
    offset = (neighbours - own[:, None]).T[:, :, None]
    slots = weights.reshape(weights.shape[0], blocks, VOXBLK)
    coef = jnp.stack(
        [
            jnp.sum(jnp.where(offset == reach, slots, 0.0), axis=0) + (1.0 if reach == 0 else 0.0)
            for reach in range(-NEIGHBOUR_REACH, NEIGHBOUR_REACH + 1)
        ]
    ).reshape(2 * NEIGHBOUR_REACH + 1, width)
    labels = lax.broadcasted_iota(jnp.int32, (noise_labels.shape[0], comps), 1)
    keep = jnp.max((labels == noise_labels[:, None]).astype(jnp.float32), axis=0, keepdims=True)
    stacked = data.reshape(rows, width)
    if rows % (16 * count) == 0 and count <= 16 and blocks > 2:
        smoothed, beta = fused(stacked, maps, coef, keep, count, sub_count)
    else:
        smoothed, beta = by_collectives(stacked, maps, coef, keep, count)
    fitted = jnp.einsum("rc,cv->rv", beta, maps, preferred_element_type=jnp.float32)
    clean = (smoothed.astype(jnp.float32) - fitted).astype(jnp.bfloat16)
    return clean.reshape(subjects, frames, width)


def solution(mesh):
    return jax.shard_map(
        local,
        mesh=mesh,
        in_specs=(
            P("groups", "map", ("vox", "sub")),
            P("groups", ("vox", "sub")),
            P(("vox", "sub"), None),
            P(None, ("vox", "sub")),
            P("groups"),
        ),
        out_specs=P("groups", "map", ("vox", "sub")),
        check_vma=False,
    )
```

```python
import functools
import jax
import jax.numpy as jnp
from jax import lax
from jax.experimental import pallas as pl
from jax.experimental.pallas import tpu as pltpu
from jax.sharding import PartitionSpec as P

VOXBLK = 128
NEIGHBOUR_REACH = 1
PIVOTS = 8
MESH = pl.DeviceIdType.MESH
HIGHEST = lax.Precision.HIGHEST
NN = (((1,), (0,)), ((), ()))
NT = (((1,), (1,)), ((), ()))
TN = (((0,), (0,)), ((), ()))


def f32_dot(a, b, dims):
    return lax.dot_general(a, b, dims, precision=HIGHEST, preferred_element_type=jnp.float32)


def swept(entries, size):
    def at(i, j):
        return entries[(min(i, j), max(i, j))]

    for p in range(size):
        inverse = 1.0 / at(p, p)
        scaled = {i: at(i, p) * inverse for i in range(size) if i != p}
        later = {}
        for i in range(size):
            for j in range(i, size):
                if i == p and j == p:
                    later[(i, j)] = -inverse
                elif i == p:
                    later[(i, j)] = scaled[j]
                elif j == p:
                    later[(i, j)] = scaled[i]
                else:
                    later[(i, j)] = at(i, j) - at(i, p) * scaled[j]
        entries = later
    return entries


def negative_inverse_small(block):
    size = block.shape[0]
    row_id = lax.broadcasted_iota(jnp.int32, (size, size), 0)
    col_id = lax.broadcasted_iota(jnp.int32, (size, size), 1)
    for first in range(0, size, PIVOTS):
        group = range(PIVOTS)
        cols = [jnp.broadcast_to(block[:, first + j : first + j + 1], (size, size)) for j in group]
        rows = [block[first + i : first + i + 1, :] for i in group]
        upper = {(i, j): cols[j][first + i : first + i + 1, :] for i in group for j in group if i <= j}
        pivots = swept(upper, PIVOTS)
        in_rows = (row_id >= first) & (row_id < first + PIVOTS)
        in_cols = (col_id >= first) & (col_id < first + PIVOTS)
        rows = [
            jnp.where(col_id[:1] == first + i, -1.0, jnp.where(in_cols[:1], 0.0, rows[i])) for i in group
        ]
        cols = [jnp.where(row_id == first + i, -1.0, jnp.where(in_rows, 0.0, cols[i])) for i in group]
        block = jnp.where(in_rows | in_cols, 0.0, block)
        for i in group:
            mixed = pivots[(0, i)] * rows[0]
            for j in group[1:]:
                mixed = mixed + pivots[(min(i, j), max(i, j))] * rows[j]
            block = block + cols[i] * mixed
    return block


def negative_inverse(gram_ref, work_ref, size, step):
    row_id = lax.broadcasted_iota(jnp.int32, (size, size), 0)
    col_id = lax.broadcasted_iota(jnp.int32, (size, size), 1)
    own_row = lax.broadcasted_iota(jnp.int32, (step, size), 0)
    own_col = lax.broadcasted_iota(jnp.int32, (step, size), 1)
    work_ref[...] = gram_ref[pl.ds(0, size), :]
    for first in range(0, size, step):
        rows = work_ref[pl.ds(first, step), :]
        select = (own_col == own_row + first).astype(jnp.float32)
        small = negative_inverse_small(rows[:, first : first + step])
        in_cols = (own_col >= first) & (own_col < first + step)
        turned = jnp.where(in_cols, -select, rows)
        update = f32_dot(turned, f32_dot(small, turned, NN), TN)
        inside = ((row_id >= first) & (row_id < first + step)) | (
            (col_id >= first) & (col_id < first + step)
        )
        work_ref[...] = jnp.where(inside, 0.0, work_ref[...]) + update


def kernel(
    count, sub_count, share, gram_share, step,
    data_ref, maps_ref, neighbour_ref, weight_ref, label_ref,
    smooth_ref, beta_ref,
    pick_ref,
    low_ref, high_ref, gram_part, gram_in, gram_all, proj_part, proj_in, work_ref, beta_all,
    halo_send, halo_recv, gsend, grecv, asend, arecv, psend, precv, bsend, brecv,
):
    comps, width = maps_ref.shape
    blocks = width // VOXBLK
    me = lax.axis_index("vox") * sub_count + lax.axis_index("sub")

    def peer(k):
        return lax.rem(me + k, count)

    def device(index):
        return {"vox": lax.div(index, sub_count), "sub": lax.rem(index, sub_count)}

    def send(src, dst, send_sem, recv_sem, index):
        copy = pltpu.make_async_remote_copy(
            src_ref=src, dst_ref=dst, send_sem=send_sem, recv_sem=recv_sem,
            device_id=device(index), device_id_type=MESH,
        )
        copy.start()
        return copy

    def part(index, size, align):
        return pl.ds(pl.multiple_of(index * size, align), size)

    barrier = pltpu.get_barrier_semaphore()
    for k in range(1, count):
        pl.semaphore_signal(barrier, inc=1, device_id=device(peer(k)), device_id_type=MESH)
    pl.semaphore_wait(barrier, count - 1)

    halo = [
        send(data_ref.at[:, pl.ds(width - VOXBLK, VOXBLK)], low_ref,
             halo_send.at[0], halo_recv.at[0], peer(1)),
        send(data_ref.at[:, pl.ds(0, VOXBLK)], high_ref,
             halo_send.at[1], halo_recv.at[1], peer(count - 1)),
    ]

    maps = maps_ref[...]
    if gram_part.shape[0] > comps:
        gram_part[pl.ds(comps, gram_part.shape[0] - comps), :] = jnp.zeros(
            (gram_part.shape[0] - comps, comps), jnp.float32
        )
    gram_part[pl.ds(0, comps), :] = lax.dot_general(maps, maps, NT, preferred_element_type=jnp.float32)
    gram_copies = [
        send(gram_part.at[part(peer(k), gram_share, 8), :], gram_in.at[k], gsend.at[k], grecv.at[k], peer(k))
        for k in range(1, count)
    ]

    slots = weight_ref.shape[0]
    own_block = me * blocks + lax.broadcasted_iota(jnp.int32, (blocks, VOXBLK), 0)
    for slot in range(slots):
        offset = jnp.broadcast_to(neighbour_ref[:, slot : slot + 1], (blocks, VOXBLK)) - own_block
        for reach in range(-NEIGHBOUR_REACH, NEIGHBOUR_REACH + 1):
            pick_ref[(reach + NEIGHBOUR_REACH) * slots + slot] = (offset == reach).astype(jnp.float32)
    comp_id = lax.broadcasted_iota(jnp.int32, (comps, label_ref.shape[1]), 0)
    hit = jnp.max((comp_id == label_ref[...]).astype(jnp.float32), axis=1, keepdims=True)
    diagonal = lax.broadcasted_iota(jnp.int32, (comps, comps), 0) == lax.broadcasted_iota(
        jnp.int32, (comps, comps), 1
    )
    keep = jnp.sum(jnp.where(diagonal, hit, 0.0), axis=0, keepdims=True)

    def columns(block):
        start = block * VOXBLK
        return pl.ds(start if isinstance(block, int) else pl.multiple_of(start, VOXBLK), VOXBLK)

    def smooth(block, low, high):
        here = columns(block)

        def weight(reach):
            place = (reach + NEIGHBOUR_REACH) * slots
            return sum(
                weight_ref[pl.ds(slot, 1), here] * pick_ref[place + slot, pl.ds(block, 1), :]
                for slot in range(slots)
            )

        total = data_ref[:, here].astype(jnp.float32) * (weight(0) + 1.0)
        total = total + low.astype(jnp.float32) * weight(-1) + high.astype(jnp.float32) * weight(1)
        smooth_ref[:, here] = total.astype(jnp.bfloat16)

    def inner(block, carry):
        smooth(block, data_ref[:, columns(block - 1)], data_ref[:, columns(block + 1)])
        return carry

    lax.fori_loop(1, blocks - 1, inner, 0)

    for copy in gram_copies:
        copy.wait()
    own = part(me, gram_share, 8)
    total = gram_part[own, :]
    for k in range(1, count):
        total = total + gram_in[k]
    gram_all[own, :] = total
    all_copies = [
        send(gram_all.at[own, :], gram_all.at[own, :], asend.at[k], arecv.at[k], peer(k))
        for k in range(1, count)
    ]

    for copy in halo:
        copy.wait()
    smooth(0, low_ref[...], data_ref[:, columns(1)])
    smooth(blocks - 1, data_ref[:, columns(blocks - 2)], high_ref[...])
    proj_part[...] = lax.dot_general(smooth_ref[...], maps, NT, preferred_element_type=jnp.float32)
    proj_copies = [
        send(proj_part.at[part(peer(k), share, 16), :], proj_in.at[k], psend.at[k], precv.at[k], peer(k))
        for k in range(1, count)
    ]

    for copy in all_copies:
        copy.wait()
    negative_inverse(gram_all, work_ref, comps, step)

    for copy in proj_copies:
        copy.wait()
    mine = part(me, share, 16)
    rhs = proj_part[mine, :]
    for k in range(1, count):
        rhs = rhs + proj_in[k]
    gram = gram_all[pl.ds(0, comps), :]
    beta = -f32_dot(rhs, work_ref[...], NN)
    left = rhs - f32_dot(beta, gram, NN)
    beta = beta - f32_dot(left, work_ref[...], NN)
    beta_all[mine, :] = jnp.where(keep > 0.0, beta, 0.0).astype(jnp.bfloat16)
    beta_copies = [
        send(beta_all.at[mine, :], beta_all.at[mine, :], bsend.at[k], brecv.at[k], peer(k))
        for k in range(1, count)
    ]
    for copy in beta_copies:
        copy.wait()
    beta_ref[...] = beta_all[...]


def fused(frames, maps, neighbours, weights, labels, count, sub_count):
    rows, width = frames.shape
    comps = maps.shape[0]
    share = rows // count
    gram_share = 8 * (-(-comps // (8 * count)))
    step = next(size for size in (40, 32, 24, 16, 8) if comps % size == 0)
    f32, bf16 = jnp.float32, jnp.bfloat16
    vmem = pl.BlockSpec(memory_space=pltpu.VMEM)
    sems = pltpu.SemaphoreType.DMA((count,))
    return pl.pallas_call(
        functools.partial(kernel, count, sub_count, share, gram_share, step),
        out_shape=(
            jax.ShapeDtypeStruct((rows, width), bf16),
            jax.ShapeDtypeStruct((rows, comps), bf16),
        ),
        in_specs=[vmem] * 5,
        out_specs=(vmem, vmem),
        scratch_shapes=[
            pltpu.VMEM(((2 * NEIGHBOUR_REACH + 1) * weights.shape[0], width // VOXBLK, VOXBLK), f32),
            pltpu.VMEM((rows, VOXBLK), bf16),
            pltpu.VMEM((rows, VOXBLK), bf16),
            pltpu.VMEM((count * gram_share, comps), f32),
            pltpu.VMEM((count, gram_share, comps), f32),
            pltpu.VMEM((count * gram_share, comps), f32),
            pltpu.VMEM((rows, comps), f32),
            pltpu.VMEM((count, share, comps), f32),
            pltpu.VMEM((comps, comps), f32),
            pltpu.VMEM((rows, comps), bf16),
            pltpu.SemaphoreType.DMA((2,)),
            pltpu.SemaphoreType.DMA((2,)),
            sems, sems, sems, sems, sems, sems, sems, sems,
        ],
        compiler_params=pltpu.CompilerParams(
            collective_id=0, has_side_effects=True, vmem_limit_bytes=48 * 1024 * 1024
        ),
    )(frames, maps, neighbours, weights, labels)


def solve_gram(gram, rhs):
    lower = jnp.linalg.cholesky(gram)
    half = lax.linalg.triangular_solve(lower, rhs, left_side=True, lower=True)
    return lax.linalg.triangular_solve(lower, half, left_side=True, lower=True, transpose_a=True)


def by_collectives(frames, maps, coef, keep, count):
    forward = [(i, (i + 1) % count) for i in range(count)]
    backward = [(target, source) for source, target in forward]
    low = lax.ppermute(frames[:, -VOXBLK:], ("vox", "sub"), forward)
    high = lax.ppermute(frames[:, :VOXBLK], ("vox", "sub"), backward)
    below = jnp.concatenate([low, frames[:, :-VOXBLK]], axis=1).astype(jnp.float32)
    above = jnp.concatenate([frames[:, VOXBLK:], high], axis=1).astype(jnp.float32)
    smoothed = frames.astype(jnp.float32) * coef[1:2] + below * coef[0:1] + above * coef[2:3]
    smoothed = smoothed.astype(jnp.bfloat16)
    gram = lax.dot_general(maps, maps, NT, preferred_element_type=jnp.float32)
    proj = lax.dot_general(maps, smoothed, NT, preferred_element_type=jnp.float32)
    gram, proj = lax.psum((gram, proj), ("vox", "sub"))
    beta = solve_gram(gram, proj).T
    return smoothed, jnp.where(keep > 0.0, beta, 0.0).astype(jnp.bfloat16)


def local(data, maps, neighbours, weights, noise_labels):
    subjects, frames, width = data.shape
    comps = maps.shape[0]
    blocks = width // VOXBLK
    rows = subjects * frames
    sub_count = lax.axis_size("sub")
    count = lax.axis_size("vox") * sub_count
    stacked = data.reshape(rows, width)
    if rows % (16 * count) == 0 and count <= 16 and blocks > 2:
        smoothed, beta = fused(
            stacked, maps, neighbours, weights, noise_labels.reshape(1, -1), count, sub_count
        )
    else:
        own = lax.axis_index(("vox", "sub")) * blocks + jnp.arange(blocks, dtype=jnp.int32)
        offset = (neighbours - own[:, None]).T[:, :, None]
        slots = weights.reshape(weights.shape[0], blocks, VOXBLK)
        coef = jnp.stack(
            [
                jnp.sum(jnp.where(offset == reach, slots, 0.0), axis=0) + (1.0 if reach == 0 else 0.0)
                for reach in range(-NEIGHBOUR_REACH, NEIGHBOUR_REACH + 1)
            ]
        ).reshape(2 * NEIGHBOUR_REACH + 1, width)
        labels = lax.broadcasted_iota(jnp.int32, (noise_labels.shape[0], comps), 1)
        keep = jnp.max((labels == noise_labels[:, None]).astype(jnp.float32), axis=0, keepdims=True)
        smoothed, beta = by_collectives(stacked, maps, coef, keep, count)
    fitted = jnp.einsum("rc,cv->rv", beta, maps, preferred_element_type=jnp.float32)
    clean = (smoothed.astype(jnp.float32) - fitted).astype(jnp.bfloat16)
    return clean.reshape(subjects, frames, width)


def solution(mesh):
    return jax.shard_map(
        local,
        mesh=mesh,
        in_specs=(
            P("groups", "map", ("vox", "sub")),
            P("groups", ("vox", "sub")),
            P(("vox", "sub"), None),
            P(None, ("vox", "sub")),
            P("groups"),
        ),
        out_specs=P("groups", "map", ("vox", "sub")),
        check_vma=False,
    )
```
